32 devices in a mesh: gx: 16 (over z, y, core), gy: 2 (over x).
Axes of the slice: x: 2, y: 2, z: 4, core: 2. Of those that a mesh axis runs over, the one named last changes fastest.
Arguments:
- scalar: float32 [128, 256, 256], P('gx', 'gy'), may hold values from -6 to 6
- velocity: float32 [3, 128, 256, 256], P(None, 'gx', 'gy'), may hold values from -4 to 4
- weights: float32 [1024, 256], replicated, may hold values from -0.03125 to 0.03125
- ray_start: int32 [128, 1024], P('gx'), may hold values from 0 to 255
- ray_length: int32 [128, 1024], P('gx'), may hold values from 1 to 256, as said below
- pixel_of_ray: int32 [1024], replicated, may hold values from 0 to 1023, each once
- observed: float32 [128, 1024], P('gx'), may hold values from 0.3 to 3
Outputs:
- images: float32 [128, 1024], P('gx', 'gy')
- grad_scalar: float32 [128, 256, 256], P('gx', 'gy')
- grad_velocity: float32 [3, 128, 256, 256], P(None, 'gx', 'gy')
The draws below stay inside these ranges and needn't reach their ends.
Inputs may be any that keep to these rules, and one draw needn't show every extreme that they name: Each ray covers ray_length consecutive y cells from ray_start, wrapping around periodically. `pixel_of_ray`: each pixel receives exactly one ray.
All inputs are finite; a program needn't handle non-finite values.
Results may differ from the reference program's by a relative error of at most 0.0003.
Values sent between devices are 32-bit elements; how exact they have to be, the bound alone decides.
A program may use at most 128 MiB of HBM per device.

```python
import math
import jax
import jax.numpy as jnp
from jax import lax

NZ = 256
R = 1024
STEPS = 3
NX = 128
NY = 256


def draw_ray_length(key, part):
    values = jax.random.randint(key, (NX, R), 1, NY + 1)
    return values.at[0, 0].set(NY).astype(jnp.int32)


def plant(array, stream_key, smallest, top_value):
    longest = array.shape.index(max(array.shape))
    spots = []
    for shift in (0, 1):
        where = [jax.random.randint(jax.random.fold_in(stream_key, axis), (), 0, length) for axis, length in enumerate(array.shape)]
        where[longest] = (where[longest] + shift) % array.shape[longest]
        spots.append(tuple(where))
    return array.at[spots[0]].set(smallest).at[spots[1]].set(top_value)


def block_levels(key, dims, cuts, low, largest):
    level, own = 1.0, jax.random.fold_in(key, 6)
    for axis_at, shards_of in cuts:
        heights = jnp.exp(jax.random.uniform(jax.random.fold_in(own, axis_at), (shards_of,), jnp.float32, low / len(cuts), largest / len(cuts)))
        level = level * jnp.repeat(heights, dims[axis_at] // shards_of).reshape([-1 if axis == axis_at else 1 for axis in range(len(dims))])
    return level


def centred(rng, dims, scale, reach, pieces=(), held_as=jnp.bfloat16):
    entries = scale * jax.random.normal(rng, dims, jnp.float32)
    if pieces:
        entries = entries * block_levels(rng, dims, pieces, -0.22, 0.18)
    return jnp.clip(entries, -reach, reach).astype(held_as)


def setup_inputs(seed: int = 0) -> dict:
    splits = jax.random.split(jax.random.key(seed), 8)
    scalar = centred(splits[0], (NX, NY, NZ), 1.0, 6.0, ((0, 16), (1, 2)), jnp.float32)
    velocity = centred(splits[1], (3, NX, NY, NZ), 1.0, 4.0, ((1, 16), (2, 2)), jnp.float32)
    weights = centred(splits[2], (R, NZ), (NY * NZ // 2) ** -0.5, 0.03125, (), jnp.float32)
    ray_start = plant(jax.random.randint(splits[3], (NX, R), 0, NY), jax.random.fold_in(splits[3], 1), 0, NY - 1).astype(jnp.int32)
    ray_length = draw_ray_length(jax.random.fold_in(splits[7], 71), 0)
    pixel_of_ray = jax.random.permutation(splits[5], R).astype(jnp.int32)
    observed = jnp.clip(jnp.exp(math.log(3.0) - 2.3025851 * jax.random.uniform(splits[6], (NX, R), jnp.float32) ** block_levels(splits[6], (NX, R), ((0, 16),), -0.2, 0.2)), 0.3, 3.0)
    return dict(scalar=scalar, velocity=velocity, weights=weights, ray_start=ray_start, ray_length=ray_length, pixel_of_ray=pixel_of_ray, observed=observed)


time_step = 0.1
diffusion = 1.0

def vertical(field):
    zeros = jnp.zeros_like(field[..., :1])
    upper = jnp.concatenate([field[..., 1:], zeros], -1)
    lower = jnp.concatenate([zeros, field[..., :-1]], -1)
    return (upper, lower)

def advance(field, velocity):
    east = jnp.roll(field, -1, 0)
    west = jnp.roll(field, 1, 0)
    north = jnp.roll(field, -1, 1)
    south = jnp.roll(field, 1, 1)
    upper, lower = vertical(field)
    laplace = east + west + north + south + upper + lower - 6.0 * field
    advect = velocity[0] * (0.5 * (east - west)) + velocity[1] * (0.5 * (north - south)) + velocity[2] * (0.5 * (upper - lower))
    return field + time_step * (diffusion * laplace - advect)

def forward(scalar, velocity):
    field = scalar
    for section in range(STEPS):
        field = advance(field, velocity)
    return field

def column_mask(start, length):
    rows_all = jnp.arange(NY, dtype=jnp.int32)
    return (jnp.mod(rows_all[:, None] - start[None, :], NY) < length[None, :]).astype(jnp.float32)

def project(field, weights, ray_start, ray_length):

    def one_column(items):
        column, start, length = items
        scores = jnp.dot(column, weights.T, precision=lax.Precision.HIGHEST, preferred_element_type=jnp.float32)
        return lax.optimization_barrier(jnp.sum(column_mask(start, length) * scores, axis=0))
    return lax.map(one_column, (field, ray_start, ray_length))

def back_project(sensitivity_ray, weights, ray_start, ray_length):

    def one_column(items):
        sens_row, start, length = items
        weighted = column_mask(start, length) * sens_row[None, :]
        return jnp.dot(weighted, weights, precision=lax.Precision.HIGHEST, preferred_element_type=jnp.float32)
    return lax.map(one_column, (sensitivity_ray, ray_start, ray_length))

def reference(scalar, velocity, weights, ray_start, ray_length, pixel_of_ray, observed):
    final = forward(scalar, velocity)
    tau_ray = project(final, weights, ray_start, ray_length)
    tau = jnp.zeros_like(tau_ray).at[:, pixel_of_ray].set(tau_ray)
    images = jnp.exp(-tau)
    sensitivity = -(images - observed) * images
    sensitivity_ray = sensitivity[:, pixel_of_ray]
    adjoint_final = back_project(sensitivity_ray, weights, ray_start, ray_length)
    unused, pullback = jax.vjp(forward, scalar, velocity)
    grad_scalar, grad_velocity = pullback(adjoint_final)
    return (images, grad_scalar, grad_velocity)
```

```python
import functools

import jax
import jax.numpy as jnp
from jax import lax
from jax.experimental import pallas as pl
from jax.experimental.pallas import tpu as pltpu
from jax.sharding import PartitionSpec as P

STEPS = 3
DT = 0.1
PAD = 8
MESH = pl.DeviceIdType.MESH
F32, BF16 = jnp.float32, jnp.bfloat16


def body(
    gx, gy,
    scalar, velocity, weights, start, length, pixel, observed,
    images, grad_scalar, grad_velocity,
    C, c3, vel, wf, wt, whi, wlo, mask, onehot, obs_ray, sens,
    A, PE, PW, PN, PS, cstage, crecv, astage, arecv, tau, taurecv,
    load_sem, xsend, xrecv, ysend, yrecv, tsend, trecv,
):
    nx, ny, nz = c3.shape
    rays = weights.shape[0]
    total_y = ny * gy
    block = rays // gy
    mx, my = lax.axis_index("gx"), lax.axis_index("gy")
    right, left = lax.rem(mx + 1, gx), lax.rem(mx + gx - 1, gx)
    north, south = lax.rem(my + 1, gy), lax.rem(my + gy - 1, gy)
    rows = pl.ds(PAD, ny)
    cut = 32

    local = [
        pltpu.make_async_copy(scalar, C.at[0, pl.ds(1, nx), rows], load_sem.at[0]),
        pltpu.make_async_copy(velocity, vel, load_sem.at[1]),
        pltpu.make_async_copy(weights, wf, load_sem.at[2]),
    ]
    for copy in local:
        copy.start()

    barrier = pltpu.get_barrier_semaphore()
    peers = [lax.rem(my + d, gy) for d in range(1, gy)]
    for who in (left, right):
        pl.semaphore_signal(barrier, inc=1, device_id=(who, my), device_id_type=MESH)
    for who in peers:
        pl.semaphore_signal(barrier, inc=1, device_id=(mx, who), device_id_type=MESH)
    pl.semaphore_wait(barrier, 2 + len(peers))

    def xcopies(k, to_right, at_right, to_left, at_left):
        return [
            pltpu.make_async_remote_copy(
                to_right, at_right, xsend.at[k, 0], xrecv.at[k, 0],
                device_id=(right, my), device_id_type=MESH),
            pltpu.make_async_remote_copy(
                to_left, at_left, xsend.at[k, 1], xrecv.at[k, 1],
                device_id=(left, my), device_id_type=MESH),
        ]

    def ycopies(k, stage, recv, n):
        return [
            pltpu.make_async_remote_copy(
                stage.at[n, 0], recv.at[n, 0], ysend.at[k, 0], yrecv.at[k, 0],
                device_id=(mx, north), device_id_type=MESH),
            pltpu.make_async_remote_copy(
                stage.at[n, 1], recv.at[n, 1], ysend.at[k, 1], yrecv.at[k, 1],
                device_id=(mx, south), device_id_type=MESH),
        ]

    cx, cy, ax, ay = [], [], [], []
    for n in range(STEPS):
        cx.append(xcopies(
            n,
            scalar.at[nx - 1] if n == 0 else C.at[n, nx, rows], C.at[n, 0, rows],
            scalar.at[0] if n == 0 else C.at[n, 1, rows], C.at[n, nx + 1, rows]))
        cy.append(ycopies(n, cstage, crecv, n))
        ax.append(xcopies(
            STEPS + n,
            PW.at[n, nx], PW.at[n, 0],
            PE.at[n, 0], PE.at[n, nx]))
        ay.append(ycopies(STEPS + n, astage, arecv, n))

    for copy in cx[0]:
        copy.start()

    def planes(lo, hi, f):
        lax.fori_loop(lo, hi, lambda i, x: (f(i), x)[1], 0)

    def edges(f):
        lax.fori_loop(0, 2, lambda t, x: (f(t * (nx - 1)), x)[1], 0)

    lane = lax.broadcasted_iota(jnp.int32, (cut, nz), 1)

    def shifts_z(up, down):
        upper = jnp.where(lane == nz - 1, 0.0, pltpu.roll(up, nz - 1, 1))
        lower = jnp.where(lane == 0, 0.0, pltpu.roll(down, 1, 1))
        return upper, lower

    def around(n, i, k):
        at = PAD + k * cut
        c = C[n, i + 1, pl.ds(at, cut), :]
        east = C[n, i + 2, pl.ds(at, cut), :]
        west = C[n, i, pl.ds(at, cut), :]
        up_y = C[n, i + 1, pl.ds(at + 1, cut), :]
        down_y = C[n, i + 1, pl.ds(at - 1, cut), :]
        upper, lower = shifts_z(c, c)
        return c, east, west, up_y, down_y, upper, lower

    def stage_c(n, i):
        cstage[n, 0, pl.ds(i, 1), :] = C[n, i + 1, pl.ds(PAD + ny - 1, 1), :]
        cstage[n, 1, pl.ds(i, 1), :] = C[n, i + 1, pl.ds(PAD, 1), :]

    def forward(n, i):
        for k in range(ny // cut):
            c, east, west, up_y, down_y, upper, lower = around(n, i, k)
            here = pl.ds(k * cut, cut)
            u, v, w = vel[0, i, here, :], vel[1, i, here, :], vel[2, i, here, :]
            lap = east + west + up_y + down_y + upper + lower - 6.0 * c
            adv = u * (east - west) + v * (up_y - down_y) + w * (upper - lower)
            new = c + DT * (lap - 0.5 * adv)
            if n < STEPS - 1:
                C[n + 1, i + 1, pl.ds(PAD + k * cut, cut), :] = new
            else:
                c3[i, here, :] = new
        if n < STEPS - 1:
            stage_c(n + 1, i)

    def make_mask(i):
        s, l = start[pl.ds(i, 1), :], length[pl.ds(i, 1), :]
        for k in range(ny // cut):
            y = my * ny + k * cut + lax.broadcasted_iota(jnp.int32, (cut, rays), 0)
            d = y - s
            d = jnp.where(d < 0, d + total_y, d)
            m = jnp.where(d < l, 1.0, 0.0).astype(BF16)
            mask[i, pl.ds(k * cut, cut), :] = m
            mask[i, pl.ds(ny + k * cut, cut), :] = m

    def make_onehot(k):
        size = 64
        p = k * size + lax.broadcasted_iota(jnp.int32, (size, rays), 0)
        onehot[pl.ds(pl.multiple_of(k * size, size), size), :] = jnp.where(
            p == pixel[...], 1.0, 0.0).astype(BF16)

    def pieces(x):
        a = x.astype(BF16).astype(F32)
        b = (x - a).astype(BF16).astype(F32)
        c = x - a - b
        return jnp.concatenate([a, b, c, jnp.zeros_like(x)], 0).astype(BF16)

    def gathered(y):
        return y[:nx] + y[nx:2 * nx] + y[2 * nx:3 * nx]

    def split_weights(k):
        size = 128
        at = pl.ds(pl.multiple_of(k * size, size), size)
        w = wf[at, :]
        hi = w.astype(BF16)
        whi[at, :] = hi
        wlo[at, :] = (w - hi.astype(F32)).astype(BF16)
        wt[:, at] = w.T

    def project(i):
        ct = c3[i].T
        hi = ct.astype(BF16)
        lo = (ct - hi.astype(F32)).astype(BF16)
        both = jnp.concatenate([hi, lo], 1)
        size = 256
        for k in range(rays // size):
            at = pl.ds(k * size, size)
            s = jnp.dot(both, mask[i, :, at], preferred_element_type=F32)
            tau[pl.ds(i, 1), at] = jnp.sum(s * wt[:, at], axis=0, keepdims=True)

    def spread(x):
        one = jnp.broadcast_to(x, (16, rays)).astype(BF16)
        return jnp.concatenate([one] * (ny // 16), 0)

    def products(n, i, k, a):
        here = pl.ds(k * cut, cut)
        u, v = vel[0, i, here, :], vel[1, i, here, :]
        ua, va = 0.5 * u * a, 0.5 * v * a
        A[n, i, here, :] = a
        PE[n, i, here, :] = a + ua
        PW[n, i + 1, here, :] = a - ua
        PN[n, i, pl.ds(PAD + k * cut, cut), :] = a + va
        PS[n, i, pl.ds(PAD + k * cut, cut), :] = a - va

    def stage_a(n, i):
        astage[n, 0, pl.ds(i, 1), :] = PS[n, i, pl.ds(PAD + ny - 1, 1), :]
        astage[n, 1, pl.ds(i, 1), :] = PN[n, i, pl.ds(PAD, 1), :]

    def back_project(t):
        his, los = [], []
        for i in (t, nx - 1 - t):
            s = sens[pl.ds(i, 1), :]
            hi = s.astype(BF16).astype(F32)
            m = mask[i, :ny, :]
            his.append(m * spread(hi))
            los.append(m * spread(s - hi))
        hi, lo = jnp.concatenate(his, 0), jnp.concatenate(los, 0)
        a = (jnp.dot(hi, whi[...], preferred_element_type=F32)
             + jnp.dot(lo, whi[...], preferred_element_type=F32)
             + jnp.dot(hi, wlo[...], preferred_element_type=F32))
        for j, i in enumerate((t, nx - 1 - t)):
            for k in range(ny // cut):
                products(0, i, k, a[j * ny + k * cut:j * ny + (k + 1) * cut])
            stage_a(0, i)

    def backward(n, i):
        for k in range(ny // cut):
            here = pl.ds(k * cut, cut)
            at = PAD + k * cut
            a = A[n, i, here, :]
            wa = 0.5 * vel[2, i, here, :] * a
            upper, lower = shifts_z(a + wa, a - wa)
            near = (PE[n, i + 1, here, :] + PW[n, i, here, :]
                    + PN[n, i, pl.ds(at + 1, cut), :] + PS[n, i, pl.ds(at - 1, cut), :]
                    + upper + lower)
            new = a + DT * (near - 6.0 * a)
            if n < STEPS - 1:
                products(n + 1, i, k, new)
            else:
                grad_scalar[i, here, :] = new
        if n < STEPS - 1:
            stage_a(n + 1, i)

    def slopes(n, m, i):
        for k in range(ny // cut):
            c, east, west, up_y, down_y, upper, lower = around(m, i, k)
            here = pl.ds(k * cut, cut)
            a = (-0.5 * DT) * A[n, i, here, :]
            for j, d in enumerate((east - west, up_y - down_y, upper - lower)):
                if n == 0:
                    grad_velocity[j, i, here, :] = a * d
                else:
                    grad_velocity[j, i, here, :] += a * d

    local[0].wait()
    planes(0, nx, functools.partial(stage_c, 0))
    for copy in cy[0]:
        copy.start()
    planes(0, nx, make_mask)
    local[1].wait()
    for n in range(STEPS):
        if n == 1:
            planes(0, rays // 64, make_onehot)
            g = jnp.dot(pieces(observed[...]), onehot[...], preferred_element_type=F32)
            obs_ray[...] = gathered(g)
            local[2].wait()
            planes(0, rays // 128, split_weights)
        for copy in cy[n]:
            copy.wait()
        for i in range(nx):
            C[n, i + 1, pl.ds(PAD - 1, 1), :] = crecv[n, 0, pl.ds(i, 1), :]
            C[n, i + 1, pl.ds(PAD + ny, 1), :] = crecv[n, 1, pl.ds(i, 1), :]
        planes(1, nx - 1, functools.partial(forward, n))
        if n == STEPS - 1:
            planes(1, nx - 1, project)
        for copy in cx[n]:
            copy.wait()
        edges(functools.partial(forward, n))
        if n < STEPS - 1:
            for copy in cx[n + 1] + cy[n + 1]:
                copy.start()
        else:
            edges(project)

    sends = [
        pltpu.make_async_remote_copy(
            tau, taurecv.at[d], tsend.at[d], trecv.at[d],
            device_id=(mx, who), device_id_type=MESH)
        for d, who in enumerate(peers)
    ]
    for copy in sends:
        copy.start()
    for copy in sends:
        copy.wait()
    depth = tau[...]
    for d in range(len(peers)):
        depth = depth + taurecv[d]
    img = jnp.exp(-depth)
    sens[...] = (obs_ray[...] - img) * img

    planes(0, 1, back_project)
    for copy in ax[0]:
        copy.start()
    planes(1, nx // 2, back_project)
    for copy in ay[0]:
        copy.start()
    own = onehot[pl.ds(pl.multiple_of(my * block, block), block), :]
    images[...] = gathered(lax.dot_general(
        pieces(img), own, (((1,), (1,)), ((), ())), preferred_element_type=F32))
    for n in range(STEPS):
        planes(0, nx, functools.partial(slopes, n, STEPS - 1 - n))
        for copy in ay[n]:
            copy.wait()
        for i in range(nx):
            PS[n, i, pl.ds(PAD - 1, 1), :] = arecv[n, 0, pl.ds(i, 1), :]
            PN[n, i, pl.ds(PAD + ny, 1), :] = arecv[n, 1, pl.ds(i, 1), :]
        planes(1, nx - 1, functools.partial(backward, n))
        for copy in ax[n]:
            copy.wait()
        edges(functools.partial(backward, n))
        if n < STEPS - 1:
            for copy in ax[n + 1] + ay[n + 1]:
                copy.start()


def per_device(gx, gy, scalar, velocity, weights, start, length, pixel, observed):
    nx, ny, nz = scalar.shape
    rays = weights.shape[0]
    vmem = pl.BlockSpec(memory_space=pltpu.VMEM)
    hbm = pl.BlockSpec(memory_space=pl.ANY)
    tall = ny + 2 * PAD
    V = pltpu.VMEM
    D = pltpu.SemaphoreType.DMA
    return pl.pallas_call(
        functools.partial(body, gx, gy),
        out_shape=(
            jax.ShapeDtypeStruct((nx, rays // gy), F32),
            jax.ShapeDtypeStruct(scalar.shape, F32),
            jax.ShapeDtypeStruct(velocity.shape, F32),
        ),
        in_specs=[hbm, hbm, hbm, vmem, vmem, vmem, vmem],
        out_specs=(vmem, vmem, vmem),
        scratch_shapes=[
            V((STEPS, nx + 2, tall, nz), F32),
            V((nx, ny, nz), F32),
            V((3, nx, ny, nz), F32),
            V((rays, nz), F32),
            V((nz, rays), F32),
            V((rays, nz), BF16),
            V((rays, nz), BF16),
            V((nx, 2 * ny, rays), BF16),
            V((rays, rays), BF16),
            V((nx, rays), F32),
            V((nx, rays), F32),
            V((STEPS, nx, ny, nz), F32),
            V((STEPS, nx + 1, ny, nz), F32),
            V((STEPS, nx + 1, ny, nz), F32),
            V((STEPS, nx, tall, nz), F32),
            V((STEPS, nx, tall, nz), F32),
            V((STEPS, 2, nx, nz), F32),
            V((STEPS, 2, nx, nz), F32),
            V((STEPS, 2, nx, nz), F32),
            V((STEPS, 2, nx, nz), F32),
            V((nx, rays), F32),
            V((gy - 1, nx, rays), F32),
            D((3,)),
            D((2 * STEPS, 2)),
            D((2 * STEPS, 2)),
            D((2 * STEPS, 2)),
            D((2 * STEPS, 2)),
            D((gy - 1,)),
            D((gy - 1,)),
        ],
        compiler_params=pltpu.CompilerParams(
            collective_id=0, has_side_effects=True, vmem_limit_bytes=60 * 2**20
        ),
    )(scalar, velocity, weights, start, length, pixel[None, :], observed)


def solution(mesh):
    in_specs = (
        P("gx", "gy", None),
        P(None, "gx", "gy", None),
        P(),
        P("gx", None),
        P("gx", None),
        P(),
        P("gx", None),
    )
    out_specs = (P("gx", "gy"), P("gx", "gy", None), P(None, "gx", "gy", None))
    return jax.shard_map(
        functools.partial(per_device, mesh.shape["gx"], mesh.shape["gy"]),
        mesh=mesh, in_specs=in_specs, out_specs=out_specs, check_vma=False,
    )
```

```python
import functools

import jax
import jax.numpy as jnp
from jax import lax
from jax.experimental import pallas as pl
from jax.experimental.pallas import tpu as pltpu
from jax.sharding import PartitionSpec as P

STEPS = 3
DT = 0.1
PAD = 8
CUT = 32
MESH = pl.DeviceIdType.MESH
F32, BF16 = jnp.float32, jnp.bfloat16


def body(
    gx, gy,
    scalar, velocity, weights, start, length, pixel, observed,
    images, grad_scalar, grad_velocity,
    C, c3, vel, wf, wt, whi, wlo, mask, onehot, obs_ray, sens,
    A, PE, PW, PN, PS, cstage, crecv, astage, arecv, tau, taurecv,
    load_sem, xsend, xrecv, ysend, yrecv, tsend, trecv,
):
    nx, ny, nz = c3.shape
    rays = weights.shape[0]
    total_y = ny * gy
    block = rays // gy
    mx, my = lax.axis_index("gx"), lax.axis_index("gy")
    right, left = lax.rem(mx + 1, gx), lax.rem(mx + gx - 1, gx)
    north, south = lax.rem(my + 1, gy), lax.rem(my + gy - 1, gy)
    rows = pl.ds(PAD, ny)
    cut = CUT

    local = [
        pltpu.make_async_copy(scalar, C.at[0, pl.ds(1, nx), rows], load_sem.at[0]),
        pltpu.make_async_copy(velocity, vel, load_sem.at[1]),
        pltpu.make_async_copy(weights, wf, load_sem.at[2]),
    ]
    for copy in local:
        copy.start()

    barrier = pltpu.get_barrier_semaphore()
    peers = [lax.rem(my + d, gy) for d in range(1, gy)]
    for who in (left, right):
        pl.semaphore_signal(barrier, inc=1, device_id=(who, my), device_id_type=MESH)
    for who in peers:
        pl.semaphore_signal(barrier, inc=1, device_id=(mx, who), device_id_type=MESH)
    pl.semaphore_wait(barrier, 2 + len(peers))

    def xcopies(s, k, to_right, at_right, to_left, at_left):
        return [
            pltpu.make_async_remote_copy(
                to_right, at_right, xsend.at[s, k, 0], xrecv.at[s, k, 0],
                device_id=(right, my), device_id_type=MESH),
            pltpu.make_async_remote_copy(
                to_left, at_left, xsend.at[s, k, 1], xrecv.at[s, k, 1],
                device_id=(left, my), device_id_type=MESH),
        ]

    def ycopies(s, stage, recv, n):
        return [[
            pltpu.make_async_remote_copy(
                stage.at[n, g, d], recv.at[n, g, d], ysend.at[s, g, d], yrecv.at[s, g, d],
                device_id=(mx, (north, south)[d]), device_id_type=MESH)
            for d in range(2)] for g in range(2)]

    started = []

    def begin(copies):
        for copy in copies:
            copy.start()
            started.append(copy)

    def arrive(copies):
        for copy in copies:
            copy.wait_recv()

    chunks = ny // cut
    order = list(range(1, chunks - 1)) + [0, chunks - 1]
    cx, cy, ax, ay = [], [], [], []
    for n in range(STEPS):
        cs, rs = [], []
        for k in range(chunks):
            here, at = pl.ds(k * cut, cut), pl.ds(PAD + k * cut, cut)
            cs.append(xcopies(
                n, k,
                scalar.at[nx - 1, here] if n == 0 else C.at[n, nx, at], C.at[n, 0, at],
                scalar.at[0, here] if n == 0 else C.at[n, 1, at], C.at[n, nx + 1, at]))
            rs.append(xcopies(
                STEPS + n, k,
                PW.at[n, nx, here], PW.at[n, 0, here],
                PE.at[n, 0, here], PE.at[n, nx, here]))
        cx.append(cs)
        ax.append(rs)
        cy.append(ycopies(n, cstage, crecv, n))
        ay.append(ycopies(STEPS + n, astage, arecv, n))

    for k in order:
        begin(cx[0][k])

    def planes(lo, hi, f):
        lax.fori_loop(lo, hi, lambda i, x: (f(i), x)[1], 0)

    def edges(f):
        lax.fori_loop(0, 2, lambda t, x: (f(t * (nx - 1)), x)[1], 0)

    inner, outer = range(1, nx - 1), (0, nx - 1)

    def rim(n, recv, copies, low, high, ids):
        arrive(copies)
        g = 0 if ids is inner else 1
        for i in ids:
            low(i, recv[n, g, 0, pl.ds(i, 1), :])
            high(i, recv[n, g, 1, pl.ds(i, 1), :])

    def rim_c(n, ids):
        def low(i, x):
            C[n, i + 1, pl.ds(PAD - 1, 1), :] = x

        def high(i, x):
            C[n, i + 1, pl.ds(PAD + ny, 1), :] = x

        rim(n, crecv, cy[n][0 if ids is inner else 1], low, high, ids)

    def rim_a(n, ids):
        def low(i, x):
            PS[n, i, pl.ds(PAD - 1, 1), :] = x

        def high(i, x):
            PN[n, i, pl.ds(PAD + ny, 1), :] = x

        rim(n, arecv, ay[n][0 if ids is inner else 1], low, high, ids)

    lane = lax.broadcasted_iota(jnp.int32, (cut, nz), 1)

    def shifts_z(up, down):
        upper = jnp.where(lane == nz - 1, 0.0, pltpu.roll(up, nz - 1, 1))
        lower = jnp.where(lane == 0, 0.0, pltpu.roll(down, 1, 1))
        return upper, lower

    def around(n, i, k):
        at = PAD + k * cut
        c = C[n, i + 1, pl.ds(at, cut), :]
        east = C[n, i + 2, pl.ds(at, cut), :]
        west = C[n, i, pl.ds(at, cut), :]
        up_y = C[n, i + 1, pl.ds(at + 1, cut), :]
        down_y = C[n, i + 1, pl.ds(at - 1, cut), :]
        upper, lower = shifts_z(c, c)
        return c, east, west, up_y, down_y, upper, lower

    def stage_c(n, ids):
        g = 0 if ids is inner else 1
        for i in ids:
            cstage[n, g, 0, pl.ds(i, 1), :] = C[n, i + 1, pl.ds(PAD + ny - 1, 1), :]
            cstage[n, g, 1, pl.ds(i, 1), :] = C[n, i + 1, pl.ds(PAD, 1), :]
        begin(cy[n][g])

    def forward(n, i, ks=range(ny // cut)):
        for k in ks:
            c, east, west, up_y, down_y, upper, lower = around(n, i, k)
            here = pl.ds(k * cut, cut)
            u, v, w = vel[0, i, here, :], vel[1, i, here, :], vel[2, i, here, :]
            lap = east + west + up_y + down_y + upper + lower - 6.0 * c
            adv = u * (east - west) + v * (up_y - down_y) + w * (upper - lower)
            new = c + DT * (lap - 0.5 * adv)
            if n < STEPS - 1:
                C[n + 1, i + 1, pl.ds(PAD + k * cut, cut), :] = new
            else:
                c3[i, here, :] = new

    def make_mask(i):
        s, l = start[pl.ds(i, 1), :], length[pl.ds(i, 1), :]
        for k in range(ny // cut):
            y = my * ny + k * cut + lax.broadcasted_iota(jnp.int32, (cut, rays), 0)
            d = y - s
            d = jnp.where(d < 0, d + total_y, d)
            m = jnp.where(d < l, 1.0, 0.0).astype(BF16)
            mask[i, pl.ds(k * cut, cut), :] = m
            mask[i, pl.ds(ny + k * cut, cut), :] = m

    def make_onehot(k):
        size = 64
        p = k * size + lax.broadcasted_iota(jnp.int32, (size, rays), 0)
        onehot[pl.ds(pl.multiple_of(k * size, size), size), :] = jnp.where(
            p == pixel[...], 1.0, 0.0).astype(BF16)

    def pieces(x):
        a = x.astype(BF16).astype(F32)
        b = (x - a).astype(BF16).astype(F32)
        c = x - a - b
        return jnp.concatenate([a, b, c, jnp.zeros_like(x)], 0).astype(BF16)

    def gathered(y):
        return y[:nx] + y[nx:2 * nx] + y[2 * nx:3 * nx]

    def split_weights(k):
        size = 128
        at = pl.ds(pl.multiple_of(k * size, size), size)
        w = wf[at, :]
        hi = w.astype(BF16)
        whi[at, :] = hi
        wlo[at, :] = (w - hi.astype(F32)).astype(BF16)
        wt[:, at] = w.T

    def project(i):
        ct = c3[i].T
        hi = ct.astype(BF16)
        lo = (ct - hi.astype(F32)).astype(BF16)
        both = jnp.concatenate([hi, lo], 1)
        size = 256
        for k in range(rays // size):
            at = pl.ds(k * size, size)
            s = jnp.dot(both, mask[i, :, at], preferred_element_type=F32)
            tau[pl.ds(i, 1), at] = jnp.sum(s * wt[:, at], axis=0, keepdims=True)

    def spread(x):
        one = jnp.broadcast_to(x, (16, rays)).astype(BF16)
        return jnp.concatenate([one] * (ny // 16), 0)

    def products(n, i, k, a):
        here = pl.ds(k * cut, cut)
        u, v = vel[0, i, here, :], vel[1, i, here, :]
        ua, va = 0.5 * u * a, 0.5 * v * a
        A[n, i, here, :] = a
        PE[n, i, here, :] = a + ua
        PW[n, i + 1, here, :] = a - ua
        PN[n, i, pl.ds(PAD + k * cut, cut), :] = a + va
        PS[n, i, pl.ds(PAD + k * cut, cut), :] = a - va

    def stage_a(n, ids):
        g = 0 if ids is inner else 1
        for i in ids:
            astage[n, g, 0, pl.ds(i, 1), :] = PS[n, i, pl.ds(PAD + ny - 1, 1), :]
            astage[n, g, 1, pl.ds(i, 1), :] = PN[n, i, pl.ds(PAD, 1), :]
        begin(ay[n][g])

    def back_project(t):
        his, los = [], []
        for i in (t, nx - 1 - t):
            s = sens[pl.ds(i, 1), :]
            hi = s.astype(BF16).astype(F32)
            m = mask[i, :ny, :]
            his.append(m * spread(hi))
            los.append(m * spread(s - hi))
        hi, lo = jnp.concatenate(his, 0), jnp.concatenate(los, 0)
        a = (jnp.dot(hi, whi[...], preferred_element_type=F32)
             + jnp.dot(lo, whi[...], preferred_element_type=F32)
             + jnp.dot(hi, wlo[...], preferred_element_type=F32))
        for j, i in enumerate((t, nx - 1 - t)):
            for k in range(ny // cut):
                products(0, i, k, a[j * ny + k * cut:j * ny + (k + 1) * cut])

    def backward(n, i, ks=range(ny // cut)):
        for k in ks:
            here = pl.ds(k * cut, cut)
            at = PAD + k * cut
            a = A[n, i, here, :]
            wa = 0.5 * vel[2, i, here, :] * a
            upper, lower = shifts_z(a + wa, a - wa)
            near = (PE[n, i + 1, here, :] + PW[n, i, here, :]
                    + PN[n, i, pl.ds(at + 1, cut), :] + PS[n, i, pl.ds(at - 1, cut), :]
                    + upper + lower)
            new = a + DT * (near - 6.0 * a)
            if n < STEPS - 1:
                products(n + 1, i, k, new)
            else:
                grad_scalar[i, here, :] = new

    def slopes(n, m, i):
        for k in range(ny // cut):
            c, east, west, up_y, down_y, upper, lower = around(m, i, k)
            here = pl.ds(k * cut, cut)
            a = (-0.5 * DT) * A[n, i, here, :]
            for j, d in enumerate((east - west, up_y - down_y, upper - lower)):
                if n == 0:
                    grad_velocity[j, i, here, :] = a * d
                else:
                    grad_velocity[j, i, here, :] += a * d

    local[0].wait()
    stage_c(0, inner)
    stage_c(0, outer)
    planes(0, nx, make_mask)
    local[1].wait()
    for n in range(STEPS):
        if n == 1:
            planes(0, rays // 64, make_onehot)
            g = jnp.dot(pieces(observed[...]), onehot[...], preferred_element_type=F32)
            obs_ray[...] = gathered(g)
            local[2].wait()
            planes(0, rays // 128, split_weights)
        rim_c(n, inner)
        planes(1, nx - 1, functools.partial(forward, n))
        if n < STEPS - 1:
            stage_c(n + 1, inner)
        else:
            planes(1, nx - 1, project)
        for k in order:
            if k == 0:
                rim_c(n, outer)
            arrive(cx[n][k])
            edges(functools.partial(forward, n, ks=(k,)))
            if n < STEPS - 1:
                begin(cx[n + 1][k])
        if n < STEPS - 1:
            stage_c(n + 1, outer)
        else:
            edges(project)

    sends = [
        pltpu.make_async_remote_copy(
            tau, taurecv.at[d], tsend.at[d], trecv.at[d],
            device_id=(mx, who), device_id_type=MESH)
        for d, who in enumerate(peers)
    ]
    for copy in sends:
        copy.start()
    for copy in sends:
        copy.wait()
    depth = tau[...]
    for d in range(len(peers)):
        depth = depth + taurecv[d]
    img = jnp.exp(-depth)
    sens[...] = (obs_ray[...] - img) * img

    planes(0, 1, back_project)
    for k in order:
        begin(ax[0][k])
    stage_a(0, outer)
    planes(1, nx // 2, back_project)
    stage_a(0, inner)
    own = onehot[pl.ds(pl.multiple_of(my * block, block), block), :]
    images[...] = gathered(lax.dot_general(
        pieces(img), own, (((1,), (1,)), ((), ())), preferred_element_type=F32))
    for n in range(STEPS):
        planes(0, nx, functools.partial(slopes, n, STEPS - 1 - n))
        rim_a(n, inner)
        planes(1, nx - 1, functools.partial(backward, n))
        if n < STEPS - 1:
            stage_a(n + 1, inner)
        for k in order:
            if k == 0:
                rim_a(n, outer)
            arrive(ax[n][k])
            edges(functools.partial(backward, n, ks=(k,)))
            if n < STEPS - 1:
                begin(ax[n + 1][k])
        if n < STEPS - 1:
            stage_a(n + 1, outer)
    for copy in started:
        copy.wait_send()


def write_out(*refs):
    count = len(refs) // 2
    sems = refs[-1]
    copies = [
        pltpu.make_async_copy(a, b, sems.at[j])
        for j, (a, b) in enumerate(zip(refs[:count], refs[count:-1]))
    ]
    for copy in copies:
        copy.start()
    for copy in copies:
        copy.wait()


def per_device(gx, gy, scalar, velocity, weights, start, length, pixel, observed):
    nx, ny, nz = scalar.shape
    rays = weights.shape[0]
    vmem = pl.BlockSpec(memory_space=pltpu.VMEM)
    hbm = pl.BlockSpec(memory_space=pl.ANY)
    tall = ny + 2 * PAD
    V = pltpu.VMEM
    D = pltpu.SemaphoreType.DMA
    shapes = ((nx, rays // gy), scalar.shape, velocity.shape)
    parts = pl.pallas_call(
        functools.partial(body, gx, gy),
        out_shape=tuple(pltpu.VMEM(x, F32) for x in shapes),
        in_specs=[hbm, hbm, hbm, vmem, vmem, vmem, vmem],
        out_specs=(vmem, vmem, vmem),
        scratch_shapes=[
            V((STEPS, nx + 2, tall, nz), F32),
            V((nx, ny, nz), F32),
            V((3, nx, ny, nz), F32),
            V((rays, nz), F32),
            V((nz, rays), F32),
            V((rays, nz), BF16),
            V((rays, nz), BF16),
            V((nx, 2 * ny, rays), BF16),
            V((rays, rays), BF16),
            V((nx, rays), F32),
            V((nx, rays), F32),
            V((STEPS, nx, ny, nz), F32),
            V((STEPS, nx + 1, ny, nz), F32),
            V((STEPS, nx + 1, ny, nz), F32),
            V((STEPS, nx, tall, nz), F32),
            V((STEPS, nx, tall, nz), F32),
            V((STEPS, 2, 2, nx, nz), F32),
            V((STEPS, 2, 2, nx, nz), F32),
            V((STEPS, 2, 2, nx, nz), F32),
            V((STEPS, 2, 2, nx, nz), F32),
            V((nx, rays), F32),
            V((gy - 1, nx, rays), F32),
            D((3,)),
            D((2 * STEPS, ny // CUT, 2)),
            D((2 * STEPS, ny // CUT, 2)),
            D((2 * STEPS, 2, 2)),
            D((2 * STEPS, 2, 2)),
            D((gy - 1,)),
            D((gy - 1,)),
        ],
        compiler_params=pltpu.CompilerParams(
            collective_id=0, has_side_effects=True, vmem_limit_bytes=50 * 2**20
        ),
    )(scalar, velocity, weights, start, length, pixel[None, :], observed)
    return pl.pallas_call(
        write_out,
        out_shape=tuple(jax.ShapeDtypeStruct(x, F32) for x in shapes),
        in_specs=[vmem] * 3,
        out_specs=(hbm,) * 3,
        scratch_shapes=[D((3,))],
        compiler_params=pltpu.CompilerParams(vmem_limit_bytes=2**20),
    )(*parts)


def solution(mesh):
    in_specs = (
        P("gx", "gy", None),
        P(None, "gx", "gy", None),
        P(),
        P("gx", None),
        P("gx", None),
        P(),
        P("gx", None),
    )
    out_specs = (P("gx", "gy"), P("gx", "gy", None), P(None, "gx", "gy", None))
    return jax.shard_map(
        functools.partial(per_device, mesh.shape["gx"], mesh.shape["gy"]),
        mesh=mesh, in_specs=in_specs, out_specs=out_specs, check_vma=False,
    )
```

```python
import functools

import jax
import jax.numpy as jnp
from jax import lax
from jax.experimental import pallas as pl
from jax.experimental.pallas import tpu as pltpu
from jax.sharding import PartitionSpec as P

STEPS = 3
DT = 0.1
PAD = 8
CUT = 32
MESH = pl.DeviceIdType.MESH
F32, BF16 = jnp.float32, jnp.bfloat16


def body(
    gx, gy,
    scalar, velocity, weights, start, length, pixel, observed,
    images, grad_scalar, grad_velocity,
    C, c3, vel, wf, wt, whi, wlo, mask, onehot, obs_ray, sens,
    A, PE, PW, PN, PS, cstage, crecv, astage, arecv, tau, taurecv,
    load_sem, xsend, xrecv, ysend, yrecv, tsend, trecv,
):
    nx, ny, nz = c3.shape
    rays = weights.shape[0]
    total_y = ny * gy
    block = rays // gy
    mx, my = lax.axis_index("gx"), lax.axis_index("gy")
    right, left = lax.rem(mx + 1, gx), lax.rem(mx + gx - 1, gx)
    north, south = lax.rem(my + 1, gy), lax.rem(my + gy - 1, gy)
    rows = pl.ds(PAD, ny)
    cut = CUT

    local = [
        pltpu.make_async_copy(scalar, C.at[0, pl.ds(1, nx), rows], load_sem.at[0]),
        pltpu.make_async_copy(velocity, vel, load_sem.at[1]),
        pltpu.make_async_copy(weights, wf, load_sem.at[2]),
    ]
    for copy in local:
        copy.start()

    barrier = pltpu.get_barrier_semaphore()
    peers = [lax.rem(my + d, gy) for d in range(1, gy)]
    for who in (left, right):
        pl.semaphore_signal(barrier, inc=1, device_id=(who, my), device_id_type=MESH)
    for who in peers:
        pl.semaphore_signal(barrier, inc=1, device_id=(mx, who), device_id_type=MESH)
    pl.semaphore_wait(barrier, 2 + len(peers))

    def xcopies(s, k, to_right, at_right, to_left, at_left):
        return [
            pltpu.make_async_remote_copy(
                to_right, at_right, xsend.at[s, k, 0], xrecv.at[s, k, 0],
                device_id=(right, my), device_id_type=MESH),
            pltpu.make_async_remote_copy(
                to_left, at_left, xsend.at[s, k, 1], xrecv.at[s, k, 1],
                device_id=(left, my), device_id_type=MESH),
        ]

    def ycopies(s, stage, recv, n):
        return [[
            pltpu.make_async_remote_copy(
                stage.at[n, g, d], recv.at[n, g, d], ysend.at[s, g, d], yrecv.at[s, g, d],
                device_id=(mx, (north, south)[d]), device_id_type=MESH)
            for d in range(2)] for g in range(2)]

    started = []

    def begin(copies):
        for copy in copies:
            copy.start()
            started.append(copy)

    def arrive(copies):
        for copy in copies:
            copy.wait_recv()

    chunks = ny // cut
    order = list(range(1, chunks - 1)) + [0, chunks - 1]
    cx, cy, ax, ay = [], [], [], []
    for n in range(STEPS):
        cs, rs = [], []
        for k in range(chunks):
            here, at = pl.ds(k * cut, cut), pl.ds(PAD + k * cut, cut)
            cs.append(xcopies(
                n, k,
                scalar.at[nx - 1, here] if n == 0 else C.at[n, nx, at], C.at[n, 0, at],
                scalar.at[0, here] if n == 0 else C.at[n, 1, at], C.at[n, nx + 1, at]))
            rs.append(xcopies(
                STEPS + n, k,
                PW.at[n, nx, here], PW.at[n, 0, here],
                PE.at[n, 0, here], PE.at[n, nx, here]))
        cx.append(cs)
        ax.append(rs)
        cy.append(ycopies(n, cstage, crecv, n))
        ay.append(ycopies(STEPS + n, astage, arecv, n))

    for k in order:
        begin(cx[0][k])

    def planes(lo, hi, f):
        lax.fori_loop(lo, hi, lambda i, x: (f(i), x)[1], 0)

    def edges(f):
        lax.fori_loop(0, 2, lambda t, x: (f(t * (nx - 1)), x)[1], 0)

    inner, outer = range(1, nx - 1), (0, nx - 1)

    def rim(n, recv, copies, low, high, ids):
        arrive(copies)
        g = 0 if ids is inner else 1
        for i in ids:
            low(i, recv[n, g, 0, pl.ds(i, 1), :])
            high(i, recv[n, g, 1, pl.ds(i, 1), :])

    def rim_c(n, ids):
        def low(i, x):
            C[n, i + 1, pl.ds(PAD - 1, 1), :] = x

        def high(i, x):
            C[n, i + 1, pl.ds(PAD + ny, 1), :] = x

        rim(n, crecv, cy[n][0 if ids is inner else 1], low, high, ids)

    def rim_a(n, ids):
        def low(i, x):
            PS[n, i, pl.ds(PAD - 1, 1), :] = x

        def high(i, x):
            PN[n, i, pl.ds(PAD + ny, 1), :] = x

        rim(n, arecv, ay[n][0 if ids is inner else 1], low, high, ids)

    lane = lax.broadcasted_iota(jnp.int32, (cut, nz), 1)

    def shifts_z(up, down):
        upper = jnp.where(lane == nz - 1, 0.0, pltpu.roll(up, nz - 1, 1))
        lower = jnp.where(lane == 0, 0.0, pltpu.roll(down, 1, 1))
        return upper, lower

    def around(n, i, k):
        at = PAD + k * cut
        c = C[n, i + 1, pl.ds(at, cut), :]
        east = C[n, i + 2, pl.ds(at, cut), :]
        west = C[n, i, pl.ds(at, cut), :]
        up_y = C[n, i + 1, pl.ds(at + 1, cut), :]
        down_y = C[n, i + 1, pl.ds(at - 1, cut), :]
        upper, lower = shifts_z(c, c)
        return c, east, west, up_y, down_y, upper, lower

    def stage_c(n, ids):
        g = 0 if ids is inner else 1
        for i in ids:
            cstage[n, g, 0, pl.ds(i, 1), :] = C[n, i + 1, pl.ds(PAD + ny - 1, 1), :]
            cstage[n, g, 1, pl.ds(i, 1), :] = C[n, i + 1, pl.ds(PAD, 1), :]
        begin(cy[n][g])

    def forward(n, i, ks=range(ny // cut)):
        for k in ks:
            c, east, west, up_y, down_y, upper, lower = around(n, i, k)
            here = pl.ds(k * cut, cut)
            u, v, w = vel[0, i, here, :], vel[1, i, here, :], vel[2, i, here, :]
            lap = east + west + up_y + down_y + upper + lower - 6.0 * c
            adv = u * (east - west) + v * (up_y - down_y) + w * (upper - lower)
            new = c + DT * (lap - 0.5 * adv)
            if n < STEPS - 1:
                C[n + 1, i + 1, pl.ds(PAD + k * cut, cut), :] = new
            else:
                c3[i, here, :] = new

    def make_mask(i):
        s, l = start[pl.ds(i, 1), :], length[pl.ds(i, 1), :]
        for k in range(ny // cut):
            y = my * ny + k * cut + lax.broadcasted_iota(jnp.int32, (cut, rays), 0)
            d = y - s
            d = jnp.where(d < 0, d + total_y, d)
            m = jnp.where(d < l, 1.0, 0.0).astype(BF16)
            mask[i, pl.ds(k * cut, cut), :] = m
            mask[i, pl.ds(ny + k * cut, cut), :] = m

    def make_onehot(k):
        size = 64
        p = k * size + lax.broadcasted_iota(jnp.int32, (size, rays), 0)
        onehot[pl.ds(pl.multiple_of(k * size, size), size), :] = jnp.where(
            p == pixel[...], 1.0, 0.0).astype(BF16)

    def pieces(x):
        a = x.astype(BF16).astype(F32)
        b = (x - a).astype(BF16).astype(F32)
        c = x - a - b
        return jnp.concatenate([a, b, c, jnp.zeros_like(x)], 0).astype(BF16)

    def gathered(y):
        return y[:nx] + y[nx:2 * nx] + y[2 * nx:3 * nx]

    def split_weights(k):
        size = 128
        at = pl.ds(pl.multiple_of(k * size, size), size)
        w = wf[at, :]
        hi = w.astype(BF16)
        whi[at, :] = hi
        wlo[at, :] = (w - hi.astype(F32)).astype(BF16)
        wt[:, at] = w.T

    def project(i):
        ct = c3[i].T
        hi = ct.astype(BF16)
        lo = (ct - hi.astype(F32)).astype(BF16)
        both = jnp.concatenate([hi, lo], 1)
        size = 256
        for k in range(rays // size):
            at = pl.ds(k * size, size)
            s = jnp.dot(both, mask[i, :, at], preferred_element_type=F32)
            tau[pl.ds(i, 1), at] = jnp.sum(s * wt[:, at], axis=0, keepdims=True)

    def spread(x):
        one = jnp.broadcast_to(x, (16, rays)).astype(BF16)
        return jnp.concatenate([one] * (ny // 16), 0)

    def products(n, i, k, a):
        here = pl.ds(k * cut, cut)
        u, v = vel[0, i, here, :], vel[1, i, here, :]
        ua, va = 0.5 * u * a, 0.5 * v * a
        A[n, i, here, :] = a
        PE[n, i, here, :] = a + ua
        PW[n, i + 1, here, :] = a - ua
        PN[n, i, pl.ds(PAD + k * cut, cut), :] = a + va
        PS[n, i, pl.ds(PAD + k * cut, cut), :] = a - va

    def stage_a(n, ids):
        g = 0 if ids is inner else 1
        for i in ids:
            astage[n, g, 0, pl.ds(i, 1), :] = PS[n, i, pl.ds(PAD + ny - 1, 1), :]
            astage[n, g, 1, pl.ds(i, 1), :] = PN[n, i, pl.ds(PAD, 1), :]
        begin(ay[n][g])

    def back_project(t):
        his, los = [], []
        for i in (t, nx - 1 - t):
            s = sens[pl.ds(i, 1), :]
            hi = s.astype(BF16).astype(F32)
            m = mask[i, :ny, :]
            his.append(m * spread(hi))
            los.append(m * spread(s - hi))
        hi, lo = jnp.concatenate(his, 0), jnp.concatenate(los, 0)
        a = (jnp.dot(hi, whi[...], preferred_element_type=F32)
             + jnp.dot(lo, whi[...], preferred_element_type=F32)
             + jnp.dot(hi, wlo[...], preferred_element_type=F32))
        for j, i in enumerate((t, nx - 1 - t)):
            for k in range(ny // cut):
                products(0, i, k, a[j * ny + k * cut:j * ny + (k + 1) * cut])

    def backward(n, i, ks=range(ny // cut)):
        for k in ks:
            here = pl.ds(k * cut, cut)
            at = PAD + k * cut
            a = A[n, i, here, :]
            wa = 0.5 * vel[2, i, here, :] * a
            upper, lower = shifts_z(a + wa, a - wa)
            near = (PE[n, i + 1, here, :] + PW[n, i, here, :]
                    + PN[n, i, pl.ds(at + 1, cut), :] + PS[n, i, pl.ds(at - 1, cut), :]
                    + upper + lower)
            new = a + DT * (near - 6.0 * a)
            if n < STEPS - 1:
                products(n + 1, i, k, new)
            else:
                grad_scalar[i, here, :] = new

    def slopes(n, m, i):
        for k in range(ny // cut):
            c, east, west, up_y, down_y, upper, lower = around(m, i, k)
            here = pl.ds(k * cut, cut)
            a = (-0.5 * DT) * A[n, i, here, :]
            for j, d in enumerate((east - west, up_y - down_y, upper - lower)):
                if n == 0:
                    grad_velocity[j, i, here, :] = a * d
                else:
                    grad_velocity[j, i, here, :] += a * d

    local[0].wait()
    stage_c(0, inner)
    stage_c(0, outer)
    planes(0, nx, make_mask)
    local[1].wait()
    for n in range(STEPS):
        if n == 1:
            planes(0, rays // 64, make_onehot)
            g = jnp.dot(pieces(observed[...]), onehot[...], preferred_element_type=F32)
            obs_ray[...] = gathered(g)
            local[2].wait()
            planes(0, rays // 128, split_weights)
        rim_c(n, inner)
        planes(1, nx - 1, functools.partial(forward, n))
        if n < STEPS - 1:
            stage_c(n + 1, inner)
        else:
            planes(1, nx - 1, project)
        for k in order:
            if k == 0:
                rim_c(n, outer)
            arrive(cx[n][k])
            edges(functools.partial(forward, n, ks=(k,)))
            if n < STEPS - 1:
                begin(cx[n + 1][k])
        if n < STEPS - 1:
            stage_c(n + 1, outer)
        else:
            edges(project)

    sends = [
        pltpu.make_async_remote_copy(
            tau, taurecv.at[d], tsend.at[d], trecv.at[d],
            device_id=(mx, who), device_id_type=MESH)
        for d, who in enumerate(peers)
    ]
    for copy in sends:
        copy.start()
    for copy in sends:
        copy.wait()
    depth = tau[...]
    for d in range(len(peers)):
        depth = depth + taurecv[d]
    img = jnp.exp(-depth)
    sens[...] = (obs_ray[...] - img) * img

    planes(0, 1, back_project)
    for k in order:
        begin(ax[0][k])
    stage_a(0, outer)
    planes(1, nx // 2, back_project)
    stage_a(0, inner)
    for n in range(STEPS):
        if n == 1:
            own = onehot[pl.ds(pl.multiple_of(my * block, block), block), :]
            images[...] = gathered(lax.dot_general(
                pieces(img), own, (((1,), (1,)), ((), ())), preferred_element_type=F32))
        for m in ((), (0,), range(1, n + 1))[min(n, 2)]:
            planes(0, nx, functools.partial(slopes, m, STEPS - 1 - m))
        rim_a(n, inner)
        planes(1, nx - 1, functools.partial(backward, n))
        if n < STEPS - 1:
            stage_a(n + 1, inner)
        for k in order:
            if k == 0:
                rim_a(n, outer)
            arrive(ax[n][k])
            edges(functools.partial(backward, n, ks=(k,)))
            if n < STEPS - 1:
                begin(ax[n + 1][k])
        if n < STEPS - 1:
            stage_a(n + 1, outer)
    for copy in started:
        copy.wait_send()


def write_out(*refs):
    count = len(refs) // 2
    sems = refs[-1]
    copies = [
        pltpu.make_async_copy(a, b, sems.at[j])
        for j, (a, b) in enumerate(zip(refs[:count], refs[count:-1]))
    ]
    for copy in copies:
        copy.start()
    for copy in copies:
        copy.wait()


def per_device(gx, gy, scalar, velocity, weights, start, length, pixel, observed):
    nx, ny, nz = scalar.shape
    rays = weights.shape[0]
    vmem = pl.BlockSpec(memory_space=pltpu.VMEM)
    hbm = pl.BlockSpec(memory_space=pl.ANY)
    tall = ny + 2 * PAD
    V = pltpu.VMEM
    D = pltpu.SemaphoreType.DMA
    shapes = ((nx, rays // gy), scalar.shape, velocity.shape)
    parts = pl.pallas_call(
        functools.partial(body, gx, gy),
        out_shape=tuple(pltpu.VMEM(x, F32) for x in shapes),
        in_specs=[hbm, hbm, hbm, vmem, vmem, vmem, vmem],
        out_specs=(vmem, vmem, vmem),
        scratch_shapes=[
            V((STEPS, nx + 2, tall, nz), F32),
            V((nx, ny, nz), F32),
            V((3, nx, ny, nz), F32),
            V((rays, nz), F32),
            V((nz, rays), F32),
            V((rays, nz), BF16),
            V((rays, nz), BF16),
            V((nx, 2 * ny, rays), BF16),
            V((rays, rays), BF16),
            V((nx, rays), F32),
            V((nx, rays), F32),
            V((STEPS, nx, ny, nz), F32),
            V((STEPS, nx + 1, ny, nz), F32),
            V((STEPS, nx + 1, ny, nz), F32),
            V((STEPS, nx, tall, nz), F32),
            V((STEPS, nx, tall, nz), F32),
            V((STEPS, 2, 2, nx, nz), F32),
            V((STEPS, 2, 2, nx, nz), F32),
            V((STEPS, 2, 2, nx, nz), F32),
            V((STEPS, 2, 2, nx, nz), F32),
            V((nx, rays), F32),
            V((gy - 1, nx, rays), F32),
            D((3,)),
            D((2 * STEPS, ny // CUT, 2)),
            D((2 * STEPS, ny // CUT, 2)),
            D((2 * STEPS, 2, 2)),
            D((2 * STEPS, 2, 2)),
            D((gy - 1,)),
            D((gy - 1,)),
        ],
        compiler_params=pltpu.CompilerParams(
            collective_id=0, has_side_effects=True, vmem_limit_bytes=50 * 2**20
        ),
    )(scalar, velocity, weights, start, length, pixel[None, :], observed)
    return pl.pallas_call(
        write_out,
        out_shape=tuple(jax.ShapeDtypeStruct(x, F32) for x in shapes),
        in_specs=[vmem] * 3,
        out_specs=(hbm,) * 3,
        scratch_shapes=[D((3,))],
        compiler_params=pltpu.CompilerParams(vmem_limit_bytes=2**20),
    )(*parts)


def solution(mesh):
    in_specs = (
        P("gx", "gy", None),
        P(None, "gx", "gy", None),
        P(),
        P("gx", None),
        P("gx", None),
        P(),
        P("gx", None),
    )
    out_specs = (P("gx", "gy"), P("gx", "gy", None), P(None, "gx", "gy", None))
    return jax.shard_map(
        functools.partial(per_device, mesh.shape["gx"], mesh.shape["gy"]),
        mesh=mesh, in_specs=in_specs, out_specs=out_specs, check_vma=False,
    )
```
